256 devices in a mesh: shot: 4 (over z_lo), rr: 4 (over x), rc: 16 (over y, z_hi, core).
Axes of the slice: x: 4, y: 4, z: 8 (z_hi: 2, z_lo: 4; z = z_hi * 4 + z_lo), core: 2. Of those that a mesh axis runs over, the one named last changes fastest.
Arguments:
- records: bfloat16 [2, 8192, 4096], P(None, ('rr', 'rc'), 'shot'), may hold values from -0.44194174 to 0.44194174
Outputs:
- point_spread: float32 [2, 4, 16, 4, 32, 4, 2048], P(None, 'rr', None, 'shot', None, None, 'rc')
The draws below stay inside these ranges and needn't reach their ends.
All inputs are finite; a program needn't handle non-finite values.
Results may differ from the reference program's by a relative error of at most 0.0003.
Values may be sent and summed in bfloat16 or wider, within the bound.
A program may use at most 128 MiB of HBM per device.

```python
import math
import jax
import jax.numpy as jnp
from jax import lax

R = 8192
SHOTS = 4096
BLOCKS = 4
STRIPS = 16
QUARTERS = 4
BLOCK = 2048
SUB = 32


def draw_records(key, part):
    key = jax.random.fold_in(key, 11)
    key_rec, key_shot, key_noise = jax.random.split(key, 3)
    receiver_gain = jnp.exp(jax.random.uniform(key_rec, (1, R, 1), jnp.float32, math.log(0.3), math.log(3.0)))
    shot_gain = jnp.exp(jax.random.uniform(key_shot, (1, 1, SHOTS), jnp.float32, math.log(0.5), math.log(2.0)))
    noise = jnp.clip(jax.random.normal(key_noise, (2, R, SHOTS), jnp.float32), -6.0, 6.0)
    scale = (2.0 * SHOTS) ** (-0.5)
    return (receiver_gain * shot_gain * noise * scale).astype(jnp.bfloat16)


def setup_inputs(seed: int = 0) -> dict:
    arg_keys = jax.random.split(jax.random.key(seed), 2)
    records = draw_records(jax.random.fold_in(arg_keys[1], 71), 0)
    return {"records": records}


def reference(records):
    real_part = records[0].astype(jnp.float32)
    imag_part = records[1].astype(jnp.float32)
    joined = jnp.concatenate([real_part, imag_part], axis=1)
    turned = jnp.concatenate([imag_part, -real_part], axis=1)
    real_gram = jnp.dot(joined, joined.T, precision=lax.Precision.HIGHEST, preferred_element_type=jnp.float32)
    imag_gram = jnp.dot(turned, joined.T, precision=lax.Precision.HIGHEST, preferred_element_type=jnp.float32)
    whole = jnp.stack([real_gram, imag_gram])
    return whole.reshape(2, BLOCKS, STRIPS, QUARTERS, SUB, BLOCKS, BLOCK)
```

```python
import jax
import jax.numpy as jnp
from jax import lax
from jax.experimental import pallas as pl
from jax.experimental.pallas import tpu as pltpu
from jax.sharding import PartitionSpec as P

MESH = pl.DeviceIdType.MESH
NT = (((1,), (1,)), ((), ()))
ROWS, SHOTS = 128, 1024
SUB = 32
PEAK = 1024.0
TINY = 1e-34
N_SEMS = 120


def kernel(x_ref, o_ref, cols, rows, w, acc0, acc1, enc_out, enc_in, top_out, top_in, ssem, rsem, lsem):
    zlo = lax.axis_index("shot")
    x = lax.axis_index("rr")
    rc = lax.axis_index("rc")
    y = rc // 4
    zhi = (rc // 2) % 2
    c = rc % 2

    def dev(x, y, zhi, zlo, c):
        return {"shot": zlo, "rr": x, "rc": y * 4 + zhi * 2 + c}

    q_odd = zlo + 1 - 2 * (zlo % 2)
    q_two = (zlo + 2) % 4
    q_three = 3 - zlo
    xs = {0: x, 1: (x + 1) % 4, -1: (x + 3) % 4, 2: (x + 2) % 4}
    ys = {0: y, 1: (y + 1) % 4, -1: (y + 3) % 4, 2: (y + 2) % 4}
    xdev = {s: dev(xs[s], y, zhi, zlo, c) for s in (1, -1)}
    ydev = {s: dev(x, ys[s], zhi, zlo, c) for s in (1, -1)}
    shot_pair = dev(x, y, zhi, q_two, c)
    other_half = dev(x, y, 1 - zhi, q_two, c)
    sum_pair = dev(x, y, zhi, q_odd, c)
    sibling = dev(x, y, zhi, zlo, 1 - c)
    partners = [xdev[1], xdev[-1], ydev[1], ydev[-1], shot_pair, other_half, sum_pair, sibling]

    barrier = pltpu.get_barrier_semaphore()
    for p in partners:
        pl.semaphore_signal(barrier, inc=1, device_id=p, device_id_type=MESH)
    pl.semaphore_wait(barrier, len(partners))

    msgs = {}

    def send(key, src, dst, to):
        i = len(msgs)
        copy = pltpu.make_async_remote_copy(
            src_ref=src, dst_ref=dst, send_sem=ssem.at[i], recv_sem=rsem.at[i], device_id=to, device_id_type=MESH
        )
        copy.start()
        msgs[key] = copy

    def got(*keys):
        for key in keys:
            msgs[key].wait_recv()

    locals_ = []

    def local(src, dst):
        copy = pltpu.make_async_copy(src, dst, lsem.at[len(locals_)])
        copy.start()
        locals_.append(copy)

    def part(q):
        return pl.ds(pl.multiple_of(q * SUB, SUB), SUB)

    def strip(zown, yy):
        half = zhi if zown else 1 - zhi
        return ys[yy] * 4 + half * 2 + c

    row_part = {0: q_odd, 1: zlo}
    there_part = {0: q_three, 1: q_two}

    def y_send(zown, g, q, src=None):
        spot = rows.at[q, g, :, strip(zown, 0)]
        src = spot if src is None else src
        for s in (1, -1):
            send(("yd", zown, g, q, s), src, spot, ydev[s])
        send(("cc", zown, g, q, 0), src, spot, sibling)

    def y_forward(zown, g, q):
        for s in (1, -1):
            got(("yd", zown, g, q, s))
            p = 0 if s == 1 else 1
            spot = rows.at[q, g, p, strip(zown, -s)]
            send(("yf", zown, g, q, s), spot, spot, ydev[s])
        for s in (1, -1):
            spot = rows.at[q, g, :, strip(zown, s)]
            send(("cc", zown, g, q, s), spot, spot, sibling)

    def y_last(zown, g, q):
        got(("yf", zown, g, q, 1), ("yf", zown, g, q, -1))
        spot = rows.at[q, g, :, strip(zown, 2)]
        send(("cc", zown, g, q, 2), spot, spot, sibling)

    order = [q_odd, q_three, q_two, zlo]
    sent_as = [q_three, q_odd, zlo, q_two]

    def x_send(i):
        spot = cols.at[x, 1, :, part(order[i])]
        for s in (1, -1):
            send(("xd", 1, s, i), spot, spot, xdev[s])

    def x_forward(i):
        for s in (1, -1):
            got(("xd", 1, s, i))
            p = 0 if s == 1 else 1
            spot = cols.at[xs[-s], 1, p, part(order[i])]
            send(("xf", 1, s, i), spot, spot, xdev[s])

    for i in range(2):
        send(("l2", i), x_ref.at[:, part(sent_as[i])], cols.at[x, 1, :, part(sent_as[i])], shot_pair)
    send(("zo", 0), x_ref.at[:, part(there_part[0])], rows.at[0, 1, :, strip(True, 0)], other_half)
    y_send(True, 0, 0, x_ref.at[:, part(row_part[0])])
    for s in (1, -1):
        send(("xd", 0, s), x_ref, cols.at[x, 0], xdev[s])
    for i in range(2, 4):
        send(("l2", i), x_ref.at[:, part(sent_as[i])], cols.at[x, 1, :, part(sent_as[i])], shot_pair)
    send(("zo", 1), x_ref.at[:, part(there_part[1])], rows.at[1, 1, :, strip(True, 0)], other_half)
    y_send(True, 0, 1, x_ref.at[:, part(row_part[1])])
    local(x_ref.at[:, part(row_part[0])], rows.at[0, 0, :, strip(True, 0)])
    local(x_ref.at[:, part(row_part[1])], rows.at[1, 0, :, strip(True, 0)])

    def build(d, g, real, imag):
        w[d, g, 0, 0:ROWS] = real
        w[d, g, 0, ROWS:] = -imag
        w[d, g, 1, 0:ROWS] = imag
        w[d, g, 1, ROWS:] = real

    def build_from(d, g, xi):
        build(d, g, cols[xi, g, 0], cols[xi, g, 1])

    build(0, 0, x_ref[0], x_ref[1])

    y_forward(True, 0, 0)
    got(("zo", 0))
    y_send(False, 1, 0)
    got(("l2", 0))
    y_send(True, 1, 0, cols.at[x, 1, :, part(row_part[0])])
    local(cols.at[x, 1, :, part(row_part[0])], rows.at[0, 1, :, strip(True, 0)])
    x_send(0)
    y_forward(True, 0, 1)
    y_forward(False, 1, 0)
    got(("l2", 1))
    send(("zr", 0), cols.at[x, 1, :, part(there_part[0])], rows.at[0, 0, :, strip(True, 0)], other_half)
    x_send(1)
    got(("zo", 1))
    y_send(False, 1, 1)
    y_forward(True, 1, 0)
    for s in (1, -1):
        got(("xd", 0, s))
        p = 0 if s == 1 else 1
        spot = cols.at[xs[-s], 0, p]
        send(("xf", 0, s), spot, spot, xdev[s])
    y_last(True, 0, 0)
    y_last(True, 0, 1)
    y_last(False, 1, 0)
    y_last(True, 1, 0)
    y_forward(False, 1, 1)
    got(("zr", 0))
    y_send(False, 0, 0)
    got(("l2", 2))
    send(("zr", 1), cols.at[x, 1, :, part(there_part[1])], rows.at[1, 0, :, strip(True, 0)], other_half)
    x_send(2)
    x_forward(0)
    x_forward(1)
    y_forward(False, 0, 0)
    got(("l2", 3))
    y_send(True, 1, 1, cols.at[x, 1, :, part(row_part[1])])
    local(cols.at[x, 1, :, part(row_part[1])], rows.at[1, 1, :, strip(True, 0)])
    x_send(3)
    build_from(0, 1, x)
    y_last(False, 0, 0)
    got(("zr", 1))
    y_send(False, 0, 1)

    def take_sibling(q):
        for zown in (True, False):
            for g in (0, 1):
                for yy in (0, 1, -1, 2):
                    got(("cc", zown, g, q, yy))

    def product(q, d):
        total = None
        for g in (0, 1):
            for p in (0, 1):
                left = rows[q, g, p].reshape(16 * SUB, SHOTS)
                term = lax.dot_general(left, w[d, g, p], NT, preferred_element_type=jnp.float32)
                total = term if total is None else total + term
        return total

    def give(d):
        acc0[...] = product(0, d)

        def look(r, top):
            return jnp.maximum(top, jnp.abs(acc0[pl.ds(r * 64, 64)]).reshape(8, 8, 256).max(axis=0))

        top = lax.fori_loop(0, 8, look, jnp.zeros((8, 256), jnp.float32)).max(axis=0, keepdims=True)
        top = jnp.maximum(top, TINY)
        top_out[d] = jnp.broadcast_to(top, (8, 256))
        scale = PEAK / top

        def code(r, _):
            at = pl.ds(pl.multiple_of(r * 64, 64), 64)
            t = acc0[at] * scale
            t2 = t * t
            t4 = t2 * t2
            t12 = t4 * t4 * t4
            enc_out[d, at] = jnp.where(t < 0, -t12, t12).astype(jnp.bfloat16)
            return 0

        lax.fori_loop(0, 8, code, 0)
        send(("ev", d), enc_out.at[d], enc_in.at[d], sum_pair)
        send(("et", d), top_out.at[d], top_in.at[d], sum_pair)

    for copy in locals_[:3]:
        copy.wait()
    take_sibling(0)
    give(0)

    y_last(False, 1, 1)
    y_forward(True, 1, 1)
    x_forward(2)
    y_forward(False, 0, 1)
    x_forward(3)
    build_from(1, 0, xs[1])
    build_from(1, 1, xs[1])
    give(1)
    y_last(True, 1, 1)
    y_last(False, 0, 1)
    build_from(2, 0, xs[-1])
    build_from(2, 1, xs[-1])
    give(2)
    for s in (1, -1):
        got(("xf", 0, s))
        for i in range(4):
            got(("xf", 1, s, i))
    build_from(3, 0, xs[2])
    build_from(3, 1, xs[2])
    give(3)

    locals_[3].wait()
    take_sibling(1)

    def keep(d, _):
        acc1[d] = product(1, d)
        return 0

    lax.fori_loop(0, 4, keep, 0)

    for d, xi in enumerate((xs[0], xs[1], xs[-1], xs[2])):
        got(("ev", d), ("et", d))
        top = top_in[d][0:1] * (1.0 / PEAK)

        def finish(r, _):
            at = pl.ds(pl.multiple_of(r * 64, 64), 64)
            u = enc_in[d, at].astype(jnp.float32)
            size = jnp.exp2(jnp.log2(jnp.abs(u)) * (1.0 / 12.0)) * top
            total = acc1[d, at] + jnp.where(u < 0, -size, size)
            for k in (0, 1):
                o_ref[pl.ds(k * 2048 + r * 256 + xi, 64, stride=4), :] = total[:, k * ROWS : (k + 1) * ROWS]
            return 0

        lax.fori_loop(0, 8, finish, 0)

    for copy in msgs.values():
        copy.wait_send()


def on_device(records):
    flat = pl.pallas_call(
        kernel,
        out_shape=jax.ShapeDtypeStruct((4096, 128), jnp.float32),
        in_specs=[pl.BlockSpec(memory_space=pltpu.VMEM)],
        out_specs=pl.BlockSpec(memory_space=pltpu.VMEM),
        scratch_shapes=[
            pltpu.VMEM((4, 2, 2, ROWS, SHOTS), jnp.bfloat16),
            pltpu.VMEM((2, 2, 2, 16, SUB, SHOTS), jnp.bfloat16),
            pltpu.VMEM((4, 2, 2, 2 * ROWS, SHOTS), jnp.bfloat16),
            pltpu.VMEM((512, 256), jnp.float32),
            pltpu.VMEM((4, 512, 256), jnp.float32),
            pltpu.VMEM((4, 512, 256), jnp.bfloat16),
            pltpu.VMEM((4, 512, 256), jnp.bfloat16),
            pltpu.VMEM((4, 8, 256), jnp.float32),
            pltpu.VMEM((4, 8, 256), jnp.float32),
            pltpu.SemaphoreType.DMA((N_SEMS,)),
            pltpu.SemaphoreType.DMA((N_SEMS,)),
            pltpu.SemaphoreType.DMA((4,)),
        ],
        compiler_params=pltpu.CompilerParams(
            collective_id=0, has_side_effects=True, vmem_limit_bytes=52 * 2**20
        ),
        cost_estimate=pl.CostEstimate(flops=8_600_000_000, bytes_accessed=3_000_000, transcendentals=1_000_000),
    )(records)
    return flat.reshape(2, 1, 16, 1, 32, 4, 128)


def solution(mesh):
    return jax.shard_map(
        on_device,
        mesh=mesh,
        in_specs=(P(None, ("rr", "rc"), "shot"),),
        out_specs=P(None, "rr", None, "shot", None, None, "rc"),
        check_vma=False,
    )
```

```python
import jax
import jax.numpy as jnp
from jax import lax
from jax.experimental import pallas as pl
from jax.experimental.pallas import tpu as pltpu
from jax.sharding import PartitionSpec as P

MESH = pl.DeviceIdType.MESH
NT = (((1,), (1,)), ((), ()))
ROWS, SHOTS = 128, 1024
SUB = 32
HALF = 8 * SUB
WIDE = 2 * ROWS
PEAK = 512.0
TINY = 1e-34
N_SEMS = 108
EV, ET = 92, 100


def kernel(x_ref, o_ref, cols, rows, w, acc0, acc1, enc_out, enc_in, top_out, top_in, ssem, rsem, lsem):
    zlo = lax.axis_index("shot")
    x = lax.axis_index("rr")
    rc = lax.axis_index("rc")
    y = rc // 4
    zhi = (rc // 2) % 2
    c = rc % 2

    def dev(x, y, zhi, zlo, c):
        return {"shot": zlo, "rr": x, "rc": y * 4 + zhi * 2 + c}

    q_odd = zlo + 1 - 2 * (zlo % 2)
    q_two = (zlo + 2) % 4
    q_three = 3 - zlo
    xs = {0: x, 1: (x + 1) % 4, -1: (x + 3) % 4, 2: (x + 2) % 4}
    ys = {0: y, 1: (y + 1) % 4, -1: (y + 3) % 4, 2: (y + 2) % 4}
    xdev = {s: dev(xs[s], y, zhi, zlo, c) for s in (1, -1)}
    ydev = {s: dev(x, ys[s], zhi, zlo, c) for s in (1, -1)}
    shot_pair = dev(x, y, zhi, q_two, c)
    other_half = dev(x, y, 1 - zhi, q_two, c)
    sum_pair = dev(x, y, zhi, q_odd, c)
    sibling = dev(x, y, zhi, zlo, 1 - c)
    partners = [xdev[1], xdev[-1], ydev[1], ydev[-1], shot_pair, other_half, sum_pair, sibling]

    barrier = pltpu.get_barrier_semaphore()
    for p in partners:
        pl.semaphore_signal(barrier, inc=1, device_id=p, device_id_type=MESH)
    pl.semaphore_wait(barrier, len(partners))

    msgs = {}

    def plan(key, src, dst, to):
        i = len(msgs)
        msgs[key] = pltpu.make_async_remote_copy(
            src_ref=src, dst_ref=dst, send_sem=ssem.at[i], recv_sem=rsem.at[i], device_id=to, device_id_type=MESH
        )

    def go(*keys):
        for key in keys:
            msgs[key].start()

    def got(*keys):
        for key in keys:
            msgs[key].wait_recv()

    def part(q):
        return pl.ds(pl.multiple_of(q * SUB, SUB), SUB)

    def strip(zown, yy):
        half = zhi if zown else 1 - zhi
        return half * 8 + ys[yy] * 2 + c

    row_part = (q_odd, zlo)
    there_part = (q_three, q_two)
    order = (q_three, q_odd, q_two, zlo)
    sent_as = (q_odd, q_three, zlo, q_two)
    here = strip(True, 0)

    for i in range(4):
        plan(("l2", i), x_ref.at[:, part(sent_as[i])], cols.at[x, 1, :, part(sent_as[i])], shot_pair)
    for q in (0, 1):
        plan(("zo", q), x_ref.at[:, part(there_part[q])], rows.at[q, 1, :, here], other_half)
        plan(("zr", q), cols.at[x, 1, :, part(there_part[q])], rows.at[q, 0, :, here], other_half)
    for s in (1, -1):
        p = 0 if s == 1 else 1
        plan(("xd", 0, s, 0), x_ref, cols.at[x, 0], xdev[s])
        spot = cols.at[xs[-s], 0, p]
        plan(("xf", 0, s, 0), spot, spot, xdev[s])
        for i in range(4):
            spot = cols.at[x, 1, :, part(order[i])]
            plan(("xd", 1, s, i), spot, spot, xdev[s])
            spot = cols.at[xs[-s], 1, p, part(order[i])]
            plan(("xf", 1, s, i), spot, spot, xdev[s])
    for zown in (True, False):
        for g in (0, 1):
            for q in (0, 1):
                spot = rows.at[q, g, :, strip(zown, 0)]
                src = spot
                if zown:
                    src = x_ref.at[:, part(row_part[q])] if g == 0 else cols.at[x, 1, :, part(row_part[q])]
                for s in (1, -1):
                    p = 0 if s == 1 else 1
                    plan(("yd", zown, g, q, s), src, spot, ydev[s])
                    forward = rows.at[q, g, p, strip(zown, -s)]
                    plan(("yf", zown, g, q, s), forward, forward, ydev[s])
                plan(("cc", zown, g, q, 0), src, spot, sibling)
                for yy in (1, -1, 2):
                    spot = rows.at[q, g, :, strip(zown, yy)]
                    plan(("cc", zown, g, q, yy), spot, spot, sibling)

    own = {
        (g, q): pltpu.make_async_copy(
            x_ref.at[:, part(row_part[q])] if g == 0 else cols.at[x, 1, :, part(row_part[q])],
            rows.at[q, g, :, here],
            lsem.at[g * 2 + q],
        )
        for g in (0, 1)
        for q in (0, 1)
    }

    def y_send(zown, g, q):
        go(("yd", zown, g, q, 1), ("yd", zown, g, q, -1), ("cc", zown, g, q, 0))

    def y_forward(zown, g, q):
        for s in (1, -1):
            got(("yd", zown, g, q, s))
            go(("yf", zown, g, q, s))
        go(("cc", zown, g, q, 1), ("cc", zown, g, q, -1))

    def y_last(zown, g, q):
        got(("yf", zown, g, q, 1), ("yf", zown, g, q, -1))
        go(("cc", zown, g, q, 2))

    def x_send(g, i):
        go(("xd", g, 1, i), ("xd", g, -1, i))

    def x_forward(g, i):
        for s in (1, -1):
            got(("xd", g, s, i))
            go(("xf", g, s, i))

    def build(d, g, real, imag):
        w[d, g, 0, 0:ROWS] = real
        w[d, g, 0, ROWS:] = -imag
        w[d, g, 1, 0:ROWS] = imag
        w[d, g, 1, ROWS:] = real

    def build_from(d, g, xi):
        build(d, g, cols[xi, g, 0], cols[xi, g, 1])

    def take_sibling(zown, q):
        for g in (0, 1):
            for yy in (0, 1, -1, 2):
                got(("cc", zown, g, q, yy))

    go(("l2", 0), ("l2", 1), ("zo", 0))
    y_send(True, 0, 0)
    x_send(0, 0)
    go(("l2", 2), ("l2", 3), ("zo", 1))
    y_send(True, 0, 1)
    own[0, 0].start()
    own[0, 1].start()
    build(0, 0, x_ref[0], x_ref[1])

    y_forward(True, 0, 0)
    got(("zo", 0))
    y_send(False, 1, 0)
    got(("l2", 0))
    go(("zr", 0))
    x_send(1, 0)
    y_forward(False, 1, 0)
    y_last(True, 0, 0)
    got(("l2", 1))
    y_send(True, 1, 0)
    own[1, 0].start()
    x_send(1, 1)
    got(("zr", 0))
    y_send(False, 0, 0)
    x_forward(0, 0)
    y_last(False, 1, 0)
    y_forward(True, 1, 0)
    build_from(1, 0, xs[1])
    got(("l2", 2))
    go(("zr", 1))
    x_send(1, 2)
    y_forward(False, 0, 0)
    y_forward(True, 0, 1)
    got(("zo", 1))
    y_send(False, 1, 1)
    y_last(True, 1, 0)
    x_forward(1, 0)
    x_forward(1, 1)
    y_last(False, 0, 0)
    build_from(2, 0, xs[-1])
    got(("l2", 3))
    y_send(True, 1, 1)
    own[1, 1].start()
    x_send(1, 3)
    build_from(0, 1, x)
    y_last(True, 0, 1)
    got(("zr", 1))
    y_send(False, 0, 1)
    own[0, 0].wait()
    own[1, 0].wait()
    take_sibling(True, 0)

    def before_1():
        take_sibling(False, 0)
        y_forward(False, 1, 1)

    def before_2():
        y_forward(True, 1, 1)
        x_forward(1, 2)
        x_forward(1, 3)
        build_from(1, 1, xs[1])

    def before_3():
        y_forward(False, 0, 1)
        y_last(False, 1, 1)

    def before_4():
        y_last(True, 1, 1)
        build_from(2, 1, xs[-1])

    def before_5():
        y_last(False, 0, 1)

    def before_6():
        for s in (1, -1):
            got(("xf", 0, s, 0))
            for i in range(4):
                got(("xf", 1, s, i))
        build_from(3, 0, xs[2])
        build_from(3, 1, xs[2])

    def product(left, d):
        total = None
        for g in (0, 1):
            for p in (0, 1):
                term = lax.dot_general(left(g, p), w[d, g, p], NT, preferred_element_type=jnp.float32)
                total = term if total is None else total + term
        return total

    def sums(i):
        copies = []
        for a, b, first in ((enc_out, enc_in, EV), (top_out, top_in, ET)):
            copies.append(
                pltpu.make_async_remote_copy(
                    src_ref=a.at[i],
                    dst_ref=b.at[i],
                    send_sem=ssem.at[first + i],
                    recv_sem=rsem.at[first + i],
                    device_id=sum_pair,
                    device_id_type=MESH,
                )
            )
        return copies

    def give(i, _):
        for k, block in ((1, before_1), (2, before_2), (3, before_3), (4, before_4), (5, before_5), (6, before_6)):
            pl.when(i == k)(block)
        d = i // 2
        half = jnp.where(i % 2 == 0, zhi, 1 - zhi)
        at = pl.ds(half * 8, 8)
        acc0[...] = product(lambda g, p: rows[0, g, p, at].reshape(HALF, SHOTS), d)

        def look(r, top):
            return jnp.maximum(top, jnp.abs(acc0[pl.ds(pl.multiple_of(r * 64, 64), 64)]).reshape(8, 8, WIDE).max(axis=0))

        top = lax.fori_loop(0, 4, look, jnp.zeros((8, WIDE), jnp.float32)).max(axis=0, keepdims=True)
        top = jnp.maximum(top, TINY)
        top_out[i] = jnp.broadcast_to(top, (8, WIDE))
        scale = PEAK / top

        def code(r, _):
            at = pl.ds(pl.multiple_of(r * 64, 64), 64)
            t = acc0[at] * scale
            t2 = t * t
            t4 = t2 * t2
            power = t4 * t4 * t4 * t2
            enc_out[i, at] = jnp.where(t < 0, -power, power).astype(jnp.bfloat16)
            return 0

        lax.fori_loop(0, 4, code, 0)
        for copy in sums(i):
            copy.start()
        return 0

    lax.fori_loop(0, 8, give, 0)

    own[0, 1].wait()
    own[1, 1].wait()
    take_sibling(True, 1)
    take_sibling(False, 1)

    def keep(d, _):
        acc1[d] = product(lambda g, p: rows[1, g, p].reshape(2 * HALF, SHOTS), d)
        return 0

    lax.fori_loop(0, 4, keep, 0)

    def finish(i, _):
        for copy in sums(i):
            copy.wait_recv()
        d = i // 2
        half = jnp.where(i % 2 == 0, zhi, 1 - zhi)
        xi = (x + d + (d // 2) * (1 - 2 * (d % 2))) % 4
        top = top_in[i][0:1] * (1.0 / PEAK)

        def add(r, _):
            u = enc_in[i, pl.ds(pl.multiple_of(r * 64, 64), 64)].astype(jnp.float32)
            size = jnp.exp2(jnp.log2(jnp.abs(u)) * (1.0 / 14.0)) * top
            at = pl.ds(pl.multiple_of(half * HALF + r * 64, 64), 64)
            total = acc1[d, at] + jnp.where(u < 0, -size, size)
            for k in (0, 1):
                o_ref[pl.ds(k * 2048 + r * 512 + half * 256 + xi, 64, stride=4), :] = total[:, k * ROWS : (k + 1) * ROWS]
            return 0

        lax.fori_loop(0, 4, add, 0)
        return 0

    lax.fori_loop(0, 8, finish, 0)

    for copy in msgs.values():
        copy.wait_send()

    def drain(i, _):
        for copy in sums(i):
            copy.wait_send()
        return 0

    lax.fori_loop(0, 8, drain, 0)


def on_device(records):
    flat = pl.pallas_call(
        kernel,
        out_shape=pltpu.VMEM((4096, 128), jnp.float32),
        in_specs=[pl.BlockSpec(memory_space=pltpu.VMEM)],
        out_specs=pl.BlockSpec(memory_space=pltpu.VMEM),
        scratch_shapes=[
            pltpu.VMEM((4, 2, 2, ROWS, SHOTS), jnp.bfloat16),
            pltpu.VMEM((2, 2, 2, 16, SUB, SHOTS), jnp.bfloat16),
            pltpu.VMEM((4, 2, 2, WIDE, SHOTS), jnp.bfloat16),
            pltpu.VMEM((HALF, WIDE), jnp.float32),
            pltpu.VMEM((4, 2 * HALF, WIDE), jnp.float32),
            pltpu.VMEM((8, HALF, WIDE), jnp.bfloat16),
            pltpu.VMEM((8, HALF, WIDE), jnp.bfloat16),
            pltpu.VMEM((8, 8, WIDE), jnp.float32),
            pltpu.VMEM((8, 8, WIDE), jnp.float32),
            pltpu.SemaphoreType.DMA((N_SEMS,)),
            pltpu.SemaphoreType.DMA((N_SEMS,)),
            pltpu.SemaphoreType.DMA((4,)),
        ],
        compiler_params=pltpu.CompilerParams(
            collective_id=0, has_side_effects=True, vmem_limit_bytes=52 * 2**20
        ),
        cost_estimate=pl.CostEstimate(flops=8_600_000_000, bytes_accessed=3_000_000, transcendentals=1_000_000),
    )(records)
    return flat.reshape(2, 1, 16, 1, 32, 4, 128)


def solution(mesh):
    return jax.shard_map(
        on_device,
        mesh=mesh,
        in_specs=(P(None, ("rr", "rc"), "shot"),),
        out_specs=P(None, "rr", None, "shot", None, None, "rc"),
        check_vma=False,
    )
```

```python
import jax
import jax.numpy as jnp
from jax import lax
from jax.experimental import pallas as pl
from jax.experimental.pallas import tpu as pltpu
from jax.sharding import PartitionSpec as P

MESH = pl.DeviceIdType.MESH
NT = (((1,), (1,)), ((), ()))
ROWS, SHOTS = 128, 1024
SUB = 32
HALF = 8 * SUB
WIDE = 2 * ROWS
PEAK = 512.0
TINY = 1e-34
N_SEMS = 142
EV, ET = 126, 134


def kernel(x_ref, o_ref, cols, rows, w, acc0, acc1, enc_out, enc_in, top_out, top_in, ssem, rsem, lsem, ready, mine):
    zlo = lax.axis_index("shot")
    x = lax.axis_index("rr")
    rc = lax.axis_index("rc")
    y = rc // 4
    zhi = (rc // 2) % 2
    c = rc % 2

    def dev(x, y, zhi, zlo, c):
        return {"shot": zlo, "rr": x, "rc": y * 4 + zhi * 2 + c}

    q_odd = zlo + 1 - 2 * (zlo % 2)
    q_two = (zlo + 2) % 4
    q_three = 3 - zlo
    xs = {0: x, 1: (x + 1) % 4, -1: (x + 3) % 4, 2: (x + 2) % 4}
    ys = {0: y, 1: (y + 1) % 4, -1: (y + 3) % 4, 2: (y + 2) % 4}
    xdev = {s: dev(xs[s], y, zhi, zlo, c) for s in (1, -1)}
    ydev = {s: dev(x, ys[s], zhi, zlo, c) for s in (1, -1)}
    shot_pair = dev(x, y, zhi, q_two, c)
    other_half = dev(x, y, 1 - zhi, q_two, c)
    sum_pair = dev(x, y, zhi, q_odd, c)
    sibling = dev(x, y, zhi, zlo, 1 - c)
    near = [xdev[1], xdev[-1], ydev[1], ydev[-1], shot_pair, sum_pair, sibling]

    barrier = pltpu.get_barrier_semaphore()
    for p in near:
        pl.semaphore_signal(barrier, inc=1, device_id=p, device_id_type=MESH)

    @pl.when(zhi == 0)
    def _():
        pl.semaphore_signal(barrier, inc=1, device_id=other_half, device_id_type=MESH)

    pl.semaphore_wait(barrier, len(near) + zhi)

    @pl.when(zhi == 1)
    def _():
        pl.semaphore_signal(ready, inc=1, device_id=other_half, device_id_type=MESH)

    msgs = {}

    def plan(key, src, dst, to):
        i = len(msgs)
        msgs[key] = pltpu.make_async_remote_copy(
            src_ref=src, dst_ref=dst, send_sem=ssem.at[i], recv_sem=rsem.at[i], device_id=to, device_id_type=MESH
        )

    def go(*keys):
        for key in keys:
            msgs[key].start()

    def got(*keys):
        for key in keys:
            msgs[key].wait_recv()

    def part(q):
        return pl.ds(pl.multiple_of(q * SUB, SUB), SUB)

    def strip(zown, yy):
        half = zhi if zown else 1 - zhi
        return half * 8 + ys[yy] * 2 + c

    row_part = (q_odd, zlo)
    there_part = (q_three, q_two)
    order = (q_three, q_odd, q_two, zlo)
    sent_as = (q_odd, q_three, zlo, q_two)
    here = strip(True, 0)

    for i in range(4):
        for p in (0, 1):
            there = cols.at[x, 1, p, part(sent_as[i])]
            plan(("l2", i, p), x_ref.at[p, part(sent_as[i])], there, shot_pair)
    for q in (0, 1):
        for p in (0, 1):
            plan(("zo", q, p), x_ref.at[p, part(there_part[q])], rows.at[q, 1, p, here], other_half)
            plan(("zr", q, p), cols.at[x, 1, p, part(there_part[q])], rows.at[q, 0, p, here], other_half)
    for s in (1, -1):
        handed = 0 if s == 1 else 1
        for p in (0, 1):
            plan(("xd", 0, s, p), x_ref.at[p], cols.at[x, 0, p], xdev[s])
        spot = cols.at[xs[-s], 0, handed]
        plan(("xf", 0, s, 0), spot, spot, xdev[s])
        for i in range(4):
            spot = cols.at[x, 1, :, part(order[i])]
            plan(("xd", 1, s, i), spot, spot, xdev[s])
            spot = cols.at[xs[-s], 1, handed, part(order[i])]
            plan(("xf", 1, s, i), spot, spot, xdev[s])

    def source(zown, g, q, p):
        if not zown:
            return rows.at[q, g, p, strip(zown, 0)]
        return x_ref.at[p, part(row_part[q])] if g == 0 else cols.at[x, 1, p, part(row_part[q])]

    for zown in (True, False):
        for g in (0, 1):
            for q in (0, 1):
                for s in (1, -1):
                    for p in (0, 1):
                        spot = rows.at[q, g, p, strip(zown, 0)]
                        plan(("yd", zown, g, q, s, p), source(zown, g, q, p), spot, ydev[s])
                    p = 0 if s == 1 else 1
                    spot = rows.at[q, g, p, strip(zown, -s)]
                    plan(("yf", zown, g, q, s), spot, spot, ydev[s])
                    spot = rows.at[q, g, p, strip(zown, 2)]
                    plan(("cc", zown, g, q, 2, p), spot, spot, sibling)
                plan(("cc", zown, g, q, 0), source(zown, g, q, slice(None)), rows.at[q, g, :, strip(zown, 0)], sibling)
                for yy in (1, -1):
                    spot = rows.at[q, g, :, strip(zown, yy)]
                    plan(("cc", zown, g, q, yy), spot, spot, sibling)

    own = {
        (g, q): pltpu.make_async_copy(
            x_ref.at[:, part(row_part[q])] if g == 0 else cols.at[x, 1, :, part(row_part[q])],
            rows.at[q, g, :, here],
            lsem.at[g * 2 + q],
        )
        for g in (0, 1)
        for q in (0, 1)
    }

    def y_send(zown, g, q, p):
        go(("yd", zown, g, q, 1, p), ("yd", zown, g, q, -1, p))
        if p == 1:
            go(("cc", zown, g, q, 0))

    def y_forward(zown, g, q):
        for s in (1, -1):
            got(("yd", zown, g, q, s, 0 if s == 1 else 1))
            go(("yf", zown, g, q, s))
        for s in (1, -1):
            got(("yd", zown, g, q, s, 1 if s == 1 else 0))
            go(("cc", zown, g, q, -s))

    def y_last(zown, g, q):
        for s in (1, -1):
            got(("yf", zown, g, q, s))
            go(("cc", zown, g, q, 2, 0 if s == 1 else 1))

    def x_send(i):
        go(("xd", 1, 1, i), ("xd", 1, -1, i))

    def x_forward(i):
        for s in (1, -1):
            got(("xd", 1, s, i))
            go(("xf", 1, s, i))

    def build(d, g, real, imag):
        w[d, g, 0, 0:ROWS] = real
        w[d, g, 0, ROWS:] = -imag
        w[d, g, 1, 0:ROWS] = imag
        w[d, g, 1, ROWS:] = real

    def build_from(d, g, xi):
        build(d, g, cols[xi, g, 0], cols[xi, g, 1])

    def take_sibling(zown, q):
        for g in (0, 1):
            got(*(("cc", zown, g, q, yy) for yy in (0, 1, -1)))
            got(("cc", zown, g, q, 2, 0), ("cc", zown, g, q, 2, 1))

    go(*(("l2", i, p) for i in (0, 1) for p in (0, 1)))

    @pl.when(zhi == 1)
    def _():
        go(("zo", 0, 0), ("zo", 0, 1))

    for p in (0, 1):
        y_send(True, 0, 0, p)
    go(("xd", 0, 1, 0), ("xd", 0, -1, 1), ("xd", 0, 1, 1), ("xd", 0, -1, 0))
    go(*(("l2", i, p) for i in (2, 3) for p in (0, 1)))
    for p in (0, 1):
        y_send(True, 0, 1, p)
    mine_copy = pltpu.make_async_copy(x_ref, mine, lsem.at[4])
    mine_copy.start()
    own[0, 0].start()
    own[0, 1].start()
    mine_copy.wait()
    build(0, 0, mine[0], mine[1])

    y_forward(True, 0, 0)

    @pl.when(zhi == 0)
    def _():
        pl.semaphore_wait(ready, 1)
        go(("zo", 0, 0), ("zo", 0, 1))

    for p in (0, 1):
        got(("zo", 0, p))
        y_send(False, 1, 0, p)
    for p in (0, 1):
        got(("l2", 0, p))
        go(("zr", 0, p))
    go(("zo", 1, 0), ("zo", 1, 1))
    x_send(0)
    y_forward(False, 1, 0)
    y_last(True, 0, 0)
    for p in (0, 1):
        got(("l2", 1, p))
        y_send(True, 1, 0, p)
    own[1, 0].start()
    x_send(1)
    for p in (0, 1):
        got(("zr", 0, p))
        y_send(False, 0, 0, p)
    got(("xd", 0, 1, 0), ("xd", 0, -1, 1))
    go(("xf", 0, 1, 0), ("xf", 0, -1, 0))
    y_last(False, 1, 0)
    y_forward(True, 1, 0)
    got(("xd", 0, 1, 1), ("xd", 0, -1, 0))
    build_from(1, 0, xs[1])
    y_forward(False, 0, 0)
    for p in (0, 1):
        got(("l2", 2, p))
        go(("zr", 1, p))
    x_send(2)
    y_last(True, 1, 0)
    y_forward(True, 0, 1)
    for p in (0, 1):
        got(("zo", 1, p))
        y_send(False, 1, 1, p)
    x_forward(0)
    x_forward(1)
    build_from(2, 0, xs[-1])
    y_last(False, 0, 0)
    for p in (0, 1):
        got(("l2", 3, p))
        y_send(True, 1, 1, p)
    own[1, 1].start()
    x_send(3)
    build_from(0, 1, x)
    own[0, 0].wait()
    own[1, 0].wait()
    take_sibling(True, 0)

    def before_1():
        y_last(True, 0, 1)
        for p in (0, 1):
            got(("zr", 1, p))
            y_send(False, 0, 1, p)
        take_sibling(False, 0)
        y_forward(False, 1, 1)

    def before_2():
        y_forward(True, 1, 1)
        x_forward(2)
        x_forward(3)
        build_from(1, 1, xs[1])

    def before_3():
        y_forward(False, 0, 1)
        y_last(False, 1, 1)

    def before_4():
        y_last(True, 1, 1)
        build_from(2, 1, xs[-1])

    def before_5():
        y_last(False, 0, 1)

    def before_6():
        for s in (1, -1):
            got(("xf", 0, s, 0))
            for i in range(4):
                got(("xf", 1, s, i))
        build_from(3, 0, xs[2])
        build_from(3, 1, xs[2])

    def product(left, d):
        total = None
        for g in (0, 1):
            for p in (0, 1):
                term = lax.dot_general(left(g, p), w[d, g, p], NT, preferred_element_type=jnp.float32)
                total = term if total is None else total + term
        return total

    def sums(i):
        copies = []
        for a, b, first in ((enc_out, enc_in, EV), (top_out, top_in, ET)):
            copies.append(
                pltpu.make_async_remote_copy(
                    src_ref=a.at[i],
                    dst_ref=b.at[i],
                    send_sem=ssem.at[first + i],
                    recv_sem=rsem.at[first + i],
                    device_id=sum_pair,
                    device_id_type=MESH,
                )
            )
        return copies

    def give(i, _):
        for k, block in ((1, before_1), (2, before_2), (3, before_3), (4, before_4), (5, before_5), (6, before_6)):
            pl.when(i == k)(block)
        d = i // 2
        half = jnp.where(i % 2 == 0, zhi, 1 - zhi)
        at = pl.ds(half * 8, 8)
        acc0[...] = product(lambda g, p: rows[0, g, p, at].reshape(HALF, SHOTS), d)

        def look(r, top):
            return jnp.maximum(top, jnp.abs(acc0[pl.ds(pl.multiple_of(r * 64, 64), 64)]).reshape(8, 8, WIDE).max(axis=0))

        top = lax.fori_loop(0, 4, look, jnp.zeros((8, WIDE), jnp.float32)).max(axis=0, keepdims=True)
        top = jnp.maximum(top, TINY)
        top_out[i] = jnp.broadcast_to(top, (8, WIDE))
        scale = PEAK / top

        def code(r, _):
            at = pl.ds(pl.multiple_of(r * 64, 64), 64)
            t = acc0[at] * scale
            t2 = t * t
            t4 = t2 * t2
            power = t4 * t4 * t4 * t2
            enc_out[i, at] = jnp.where(t < 0, -power, power).astype(jnp.bfloat16)
            return 0

        lax.fori_loop(0, 4, code, 0)
        for copy in sums(i):
            copy.start()
        return 0

    lax.fori_loop(0, 8, give, 0)

    own[0, 1].wait()
    own[1, 1].wait()
    take_sibling(True, 1)
    take_sibling(False, 1)

    def keep(d, _):
        acc1[d] = product(lambda g, p: rows[1, g, p].reshape(2 * HALF, SHOTS), d)
        return 0

    lax.fori_loop(0, 4, keep, 0)

    for copy in msgs.values():
        copy.wait_send()

    def finish(i, _):
        for copy in sums(i):
            copy.wait_recv()
        d = i // 2
        half = jnp.where(i % 2 == 0, zhi, 1 - zhi)
        xi = (x + d + (d // 2) * (1 - 2 * (d % 2))) % 4
        top = top_in[i][0:1] * (1.0 / PEAK)

        def add(r, _):
            u = enc_in[i, pl.ds(pl.multiple_of(r * 64, 64), 64)].astype(jnp.float32)
            size = jnp.exp2(jnp.log2(jnp.abs(u)) * (1.0 / 14.0)) * top
            at = pl.ds(pl.multiple_of(half * HALF + r * 64, 64), 64)
            total = acc1[d, at] + jnp.where(u < 0, -size, size)
            for k in (0, 1):
                o_ref[pl.ds(k * 2048 + r * 512 + half * 256 + xi, 64, stride=4), :] = total[:, k * ROWS : (k + 1) * ROWS]
            return 0

        lax.fori_loop(0, 4, add, 0)
        return 0

    lax.fori_loop(0, 8, finish, 0)

    def drain(i, _):
        for copy in sums(i):
            copy.wait_send()
        return 0

    lax.fori_loop(0, 8, drain, 0)


def on_device(records):
    flat = pl.pallas_call(
        kernel,
        out_shape=pltpu.VMEM((4096, 128), jnp.float32),
        in_specs=[pl.BlockSpec(memory_space=pltpu.HBM)],
        out_specs=pl.BlockSpec(memory_space=pltpu.VMEM),
        scratch_shapes=[
            pltpu.VMEM((4, 2, 2, ROWS, SHOTS), jnp.bfloat16),
            pltpu.VMEM((2, 2, 2, 16, SUB, SHOTS), jnp.bfloat16),
            pltpu.VMEM((4, 2, 2, WIDE, SHOTS), jnp.bfloat16),
            pltpu.VMEM((HALF, WIDE), jnp.float32),
            pltpu.VMEM((4, 2 * HALF, WIDE), jnp.float32),
            pltpu.VMEM((8, HALF, WIDE), jnp.bfloat16),
            pltpu.VMEM((8, HALF, WIDE), jnp.bfloat16),
            pltpu.VMEM((8, 8, WIDE), jnp.float32),
            pltpu.VMEM((8, 8, WIDE), jnp.float32),
            pltpu.SemaphoreType.DMA((N_SEMS,)),
            pltpu.SemaphoreType.DMA((N_SEMS,)),
            pltpu.SemaphoreType.DMA((5,)),
            pltpu.SemaphoreType.REGULAR,
            pltpu.VMEM((2, ROWS, SHOTS), jnp.bfloat16),
        ],
        compiler_params=pltpu.CompilerParams(
            collective_id=0, has_side_effects=True, vmem_limit_bytes=60 * 2**20
        ),
        cost_estimate=pl.CostEstimate(flops=8_600_000_000, bytes_accessed=3_000_000, transcendentals=1_000_000),
    )(records)
    return flat.reshape(2, 1, 16, 1, 32, 4, 128)


def solution(mesh):
    return jax.shard_map(
        on_device,
        mesh=mesh,
        in_specs=(P(None, ("rr", "rc"), "shot"),),
        out_specs=P(None, "rr", None, "shot", None, None, "rc"),
        check_vma=False,
    )
```

```python
import jax
import jax.numpy as jnp
from jax import lax
from jax.experimental import pallas as pl
from jax.experimental.pallas import tpu as pltpu
from jax.sharding import PartitionSpec as P

MESH = pl.DeviceIdType.MESH
NT = (((1,), (1,)), ((), ()))
ROWS, SHOTS = 128, 1024
SUB = 32
HALF = 8 * SUB
WIDE = 2 * ROWS
PEAK = 512.0
TINY = 1e-34
N_SEMS = 142
EV, ET = 126, 134


def kernel(x_ref, o_ref, cols, rows, w, acc0, acc1, enc_out, enc_in, top_out, top_in, ssem, rsem, lsem, ready, mine):
    zlo = lax.axis_index("shot")
    x = lax.axis_index("rr")
    rc = lax.axis_index("rc")
    y = rc // 4
    zhi = (rc // 2) % 2
    c = rc % 2

    def dev(x, y, zhi, zlo, c):
        return {"shot": zlo, "rr": x, "rc": y * 4 + zhi * 2 + c}

    q_odd = zlo + 1 - 2 * (zlo % 2)
    q_two = (zlo + 2) % 4
    q_three = 3 - zlo
    xs = {0: x, 1: (x + 1) % 4, -1: (x + 3) % 4, 2: (x + 2) % 4}
    ys = {0: y, 1: (y + 1) % 4, -1: (y + 3) % 4, 2: (y + 2) % 4}
    xdev = {s: dev(xs[s], y, zhi, zlo, c) for s in (1, -1)}
    ydev = {s: dev(x, ys[s], zhi, zlo, c) for s in (1, -1)}
    shot_pair = dev(x, y, zhi, q_two, c)
    other_half = dev(x, y, 1 - zhi, q_two, c)
    sum_pair = dev(x, y, zhi, q_odd, c)
    sibling = dev(x, y, zhi, zlo, 1 - c)
    near = [xdev[1], xdev[-1], ydev[1], ydev[-1], shot_pair, sum_pair, sibling]

    barrier = pltpu.get_barrier_semaphore()
    for p in near:
        pl.semaphore_signal(barrier, inc=1, device_id=p, device_id_type=MESH)

    @pl.when(zhi == 0)
    def _():
        pl.semaphore_signal(barrier, inc=1, device_id=other_half, device_id_type=MESH)

    pl.semaphore_wait(barrier, len(near) + zhi)

    @pl.when(zhi == 1)
    def _():
        pl.semaphore_signal(ready, inc=1, device_id=other_half, device_id_type=MESH)

    msgs = {}

    def plan(key, src, dst, to):
        i = len(msgs)
        msgs[key] = pltpu.make_async_remote_copy(
            src_ref=src, dst_ref=dst, send_sem=ssem.at[i], recv_sem=rsem.at[i], device_id=to, device_id_type=MESH
        )

    def go(*keys):
        for key in keys:
            msgs[key].start()

    def got(*keys):
        for key in keys:
            msgs[key].wait_recv()

    def part(q):
        return pl.ds(pl.multiple_of(q * SUB, SUB), SUB)

    def strip(zown, yy):
        half = zhi if zown else 1 - zhi
        return half * 8 + ys[yy] * 2 + c

    row_part = (q_odd, zlo)
    there_part = (q_three, q_two)
    order = (q_three, q_odd, q_two, zlo)
    sent_as = (q_odd, q_three, zlo, q_two)
    here = strip(True, 0)

    for i in range(4):
        for p in (0, 1):
            there = cols.at[x, 1, p, part(sent_as[i])]
            plan(("l2", i, p), x_ref.at[p, part(sent_as[i])], there, shot_pair)
    for q in (0, 1):
        for p in (0, 1):
            plan(("zo", q, p), x_ref.at[p, part(there_part[q])], rows.at[q, 1, p, here], other_half)
            plan(("zr", q, p), cols.at[x, 1, p, part(there_part[q])], rows.at[q, 0, p, here], other_half)
    for s in (1, -1):
        handed = 0 if s == 1 else 1
        for p in (0, 1):
            plan(("xd", 0, s, p), x_ref.at[p], cols.at[x, 0, p], xdev[s])
        spot = cols.at[xs[-s], 0, handed]
        plan(("xf", 0, s, 0), spot, spot, xdev[s])
        for i in range(4):
            spot = cols.at[x, 1, :, part(order[i])]
            plan(("xd", 1, s, i), spot, spot, xdev[s])
            spot = cols.at[xs[-s], 1, handed, part(order[i])]
            plan(("xf", 1, s, i), spot, spot, xdev[s])

    def source(zown, g, q, p):
        if not zown:
            return rows.at[q, g, p, strip(zown, 0)]
        return x_ref.at[p, part(row_part[q])] if g == 0 else cols.at[x, 1, p, part(row_part[q])]

    for zown in (True, False):
        for g in (0, 1):
            for q in (0, 1):
                for s in (1, -1):
                    for p in (0, 1):
                        spot = rows.at[q, g, p, strip(zown, 0)]
                        plan(("yd", zown, g, q, s, p), source(zown, g, q, p), spot, ydev[s])
                    p = 0 if s == 1 else 1
                    spot = rows.at[q, g, p, strip(zown, -s)]
                    plan(("yf", zown, g, q, s), spot, spot, ydev[s])
                    spot = rows.at[q, g, p, strip(zown, 2)]
                    plan(("cc", zown, g, q, 2, p), spot, spot, sibling)
                plan(("cc", zown, g, q, 0), source(zown, g, q, slice(None)), rows.at[q, g, :, strip(zown, 0)], sibling)
                for yy in (1, -1):
                    spot = rows.at[q, g, :, strip(zown, yy)]
                    plan(("cc", zown, g, q, yy), spot, spot, sibling)

    own = {
        (g, q): pltpu.make_async_copy(
            x_ref.at[:, part(row_part[q])] if g == 0 else cols.at[x, 1, :, part(row_part[q])],
            rows.at[q, g, :, here],
            lsem.at[g * 2 + q],
        )
        for g in (0, 1)
        for q in (0, 1)
    }

    def y_send(zown, g, q, p):
        go(("yd", zown, g, q, 1, p), ("yd", zown, g, q, -1, p))
        if p == 1:
            go(("cc", zown, g, q, 0))

    def y_forward(zown, g, q):
        for s in (1, -1):
            got(("yd", zown, g, q, s, 0 if s == 1 else 1))
            go(("yf", zown, g, q, s))
        for s in (1, -1):
            got(("yd", zown, g, q, s, 1 if s == 1 else 0))
            go(("cc", zown, g, q, -s))

    def y_last(zown, g, q):
        for s in (1, -1):
            got(("yf", zown, g, q, s))
            go(("cc", zown, g, q, 2, 0 if s == 1 else 1))

    def x_send(i):
        go(("xd", 1, 1, i), ("xd", 1, -1, i))

    def x_forward(i):
        for s in (1, -1):
            got(("xd", 1, s, i))
            go(("xf", 1, s, i))

    def build(d, g, real, imag):
        w[d, g, 0, 0:ROWS] = real
        w[d, g, 0, ROWS:] = -imag
        w[d, g, 1, 0:ROWS] = imag
        w[d, g, 1, ROWS:] = real

    def build_from(d, g, xi):
        build(d, g, cols[xi, g, 0], cols[xi, g, 1])

    def take_sibling(zown, q):
        for g in (0, 1):
            got(*(("cc", zown, g, q, yy) for yy in (0, 1, -1)))
            got(("cc", zown, g, q, 2, 0), ("cc", zown, g, q, 2, 1))

    go(*(("l2", i, p) for i in (0, 1) for p in (0, 1)))

    @pl.when(zhi == 1)
    def _():
        go(("zo", 0, 0), ("zo", 0, 1))

    for p in (0, 1):
        y_send(True, 0, 0, p)
    go(("xd", 0, 1, 0), ("xd", 0, -1, 1), ("xd", 0, 1, 1), ("xd", 0, -1, 0))
    go(*(("l2", i, p) for i in (2, 3) for p in (0, 1)))
    for p in (0, 1):
        y_send(True, 0, 1, p)
    mine_copy = pltpu.make_async_copy(x_ref, mine, lsem.at[4])
    mine_copy.start()
    own[0, 0].start()
    own[0, 1].start()
    mine_copy.wait()
    build(0, 0, mine[0], mine[1])

    y_forward(True, 0, 0)

    @pl.when(zhi == 0)
    def _():
        pl.semaphore_wait(ready, 1)
        go(("zo", 0, 0), ("zo", 0, 1))

    for p in (0, 1):
        got(("zo", 0, p))
        y_send(False, 1, 0, p)
    for p in (0, 1):
        got(("l2", 0, p))
        go(("zr", 0, p))
    go(("zo", 1, 0), ("zo", 1, 1))
    x_send(0)
    y_forward(False, 1, 0)
    y_last(True, 0, 0)
    got(("xd", 0, 1, 0), ("xd", 0, -1, 1))
    go(("xf", 0, 1, 0), ("xf", 0, -1, 0))
    for p in (0, 1):
        got(("l2", 1, p))
        y_send(True, 1, 0, p)
    own[1, 0].start()
    x_send(1)
    for p in (0, 1):
        got(("zr", 0, p))
        y_send(False, 0, 0, p)
    y_last(False, 1, 0)
    y_forward(True, 1, 0)
    got(("xd", 0, 1, 1), ("xd", 0, -1, 0))
    build_from(1, 0, xs[1])
    y_forward(False, 0, 0)
    for p in (0, 1):
        got(("l2", 2, p))
        go(("zr", 1, p))
    x_send(2)
    y_last(True, 1, 0)
    y_forward(True, 0, 1)
    for p in (0, 1):
        got(("zo", 1, p))
        y_send(False, 1, 1, p)
    x_forward(0)
    x_forward(1)
    build_from(2, 0, xs[-1])
    for p in (0, 1):
        got(("l2", 3, p))
        y_send(True, 1, 1, p)
    own[1, 1].start()
    x_send(3)
    build_from(0, 1, x)
    own[0, 0].wait()
    own[1, 0].wait()
    take_sibling(True, 0)

    def before_1():
        y_last(False, 0, 0)
        y_last(True, 0, 1)
        for p in (0, 1):
            got(("zr", 1, p))
            y_send(False, 0, 1, p)
        take_sibling(False, 0)
        y_forward(False, 1, 1)

    def before_2():
        y_forward(True, 1, 1)
        x_forward(2)
        x_forward(3)
        build_from(1, 1, xs[1])

    def before_3():
        y_forward(False, 0, 1)

    def before_4():
        build_from(2, 1, xs[-1])

    def before_5():
        y_last(False, 1, 1)

    def before_6():
        for s in (1, -1):
            got(("xf", 0, s, 0))
            for i in range(4):
                got(("xf", 1, s, i))
        build_from(3, 0, xs[2])
        build_from(3, 1, xs[2])

    def product(left, d):
        total = None
        for g in (0, 1):
            for p in (0, 1):
                term = lax.dot_general(left(g, p), w[d, g, p], NT, preferred_element_type=jnp.float32)
                total = term if total is None else total + term
        return total

    def sums(i):
        copies = []
        for a, b, first in ((enc_out, enc_in, EV), (top_out, top_in, ET)):
            copies.append(
                pltpu.make_async_remote_copy(
                    src_ref=a.at[i],
                    dst_ref=b.at[i],
                    send_sem=ssem.at[first + i],
                    recv_sem=rsem.at[first + i],
                    device_id=sum_pair,
                    device_id_type=MESH,
                )
            )
        return copies

    def give(i, _):
        for k, block in ((1, before_1), (2, before_2), (3, before_3), (4, before_4), (5, before_5), (6, before_6)):
            pl.when(i == k)(block)
        d = i // 2
        half = jnp.where(i % 2 == 0, zhi, 1 - zhi)
        at = pl.ds(half * 8, 8)
        acc0[...] = product(lambda g, p: rows[0, g, p, at].reshape(HALF, SHOTS), d)

        def look(r, top):
            return jnp.maximum(top, jnp.abs(acc0[pl.ds(pl.multiple_of(r * 64, 64), 64)]).reshape(8, 8, WIDE).max(axis=0))

        top = lax.fori_loop(0, 4, look, jnp.zeros((8, WIDE), jnp.float32)).max(axis=0, keepdims=True)
        top = jnp.maximum(top, TINY)
        top_out[i] = top
        scale = PEAK / top

        def code(r, _):
            at = pl.ds(pl.multiple_of(r * 64, 64), 64)
            t = acc0[at] * scale
            t2 = t * t
            t4 = t2 * t2
            power = t4 * t4 * t4 * t2
            enc_out[i, at] = jnp.where(t < 0, -power, power).astype(jnp.bfloat16)
            return 0

        lax.fori_loop(0, 4, code, 0)
        for copy in sums(i):
            copy.start()
        return 0

    lax.fori_loop(0, 8, give, 0)

    y_last(True, 1, 1)
    y_last(False, 0, 1)
    own[0, 1].wait()
    own[1, 1].wait()
    take_sibling(True, 1)
    take_sibling(False, 1)

    def keep(d, _):
        acc1[d] = product(lambda g, p: rows[1, g, p].reshape(2 * HALF, SHOTS), d)
        return 0

    lax.fori_loop(0, 4, keep, 0)

    for copy in msgs.values():
        copy.wait_send()

    def finish(i, _):
        for copy in sums(i):
            copy.wait_recv()
        d = i // 2
        half = jnp.where(i % 2 == 0, zhi, 1 - zhi)
        xi = (x + d + (d // 2) * (1 - 2 * (d % 2))) % 4
        top = top_in[i] * (1.0 / PEAK)

        def add(r, _):
            u = enc_in[i, pl.ds(pl.multiple_of(r * 64, 64), 64)].astype(jnp.float32)
            size = jnp.exp2(jnp.log2(jnp.abs(u)) * (1.0 / 14.0)) * top
            at = pl.ds(pl.multiple_of(half * HALF + r * 64, 64), 64)
            total = acc1[d, at] + jnp.where(u < 0, -size, size)
            for k in (0, 1):
                o_ref[pl.ds(k * 2048 + r * 512 + half * 256 + xi, 64, stride=4), :] = total[:, k * ROWS : (k + 1) * ROWS]
            return 0

        lax.fori_loop(0, 4, add, 0)
        return 0

    lax.fori_loop(0, 8, finish, 0)

    def drain(i, _):
        for copy in sums(i):
            copy.wait_send()
        return 0

    lax.fori_loop(0, 8, drain, 0)


def on_device(records):
    flat = pl.pallas_call(
        kernel,
        out_shape=pltpu.VMEM((4096, 128), jnp.float32),
        in_specs=[pl.BlockSpec(memory_space=pltpu.HBM)],
        out_specs=pl.BlockSpec(memory_space=pltpu.VMEM),
        scratch_shapes=[
            pltpu.VMEM((4, 2, 2, ROWS, SHOTS), jnp.bfloat16),
            pltpu.VMEM((2, 2, 2, 16, SUB, SHOTS), jnp.bfloat16),
            pltpu.VMEM((4, 2, 2, WIDE, SHOTS), jnp.bfloat16),
            pltpu.VMEM((HALF, WIDE), jnp.float32),
            pltpu.VMEM((4, 2 * HALF, WIDE), jnp.float32),
            pltpu.VMEM((8, HALF, WIDE), jnp.bfloat16),
            pltpu.VMEM((8, HALF, WIDE), jnp.bfloat16),
            pltpu.VMEM((8, 1, WIDE), jnp.float32),
            pltpu.VMEM((8, 1, WIDE), jnp.float32),
            pltpu.SemaphoreType.DMA((N_SEMS,)),
            pltpu.SemaphoreType.DMA((N_SEMS,)),
            pltpu.SemaphoreType.DMA((5,)),
            pltpu.SemaphoreType.REGULAR,
            pltpu.VMEM((2, ROWS, SHOTS), jnp.bfloat16),
        ],
        compiler_params=pltpu.CompilerParams(
            collective_id=0, has_side_effects=True, vmem_limit_bytes=60 * 2**20
        ),
        cost_estimate=pl.CostEstimate(flops=8_600_000_000, bytes_accessed=3_000_000, transcendentals=1_000_000),
    )(records)
    return flat.reshape(2, 1, 16, 1, 32, 4, 128)


def solution(mesh):
    return jax.shard_map(
        on_device,
        mesh=mesh,
        in_specs=(P(None, ("rr", "rc"), "shot"),),
        out_specs=P(None, "rr", None, "shot", None, None, "rc"),
        check_vma=False,
    )
```

```python
import jax
import jax.numpy as jnp
from jax import lax
from jax.experimental import pallas as pl
from jax.experimental.pallas import tpu as pltpu
from jax.sharding import PartitionSpec as P

MESH = pl.DeviceIdType.MESH
NT = (((1,), (1,)), ((), ()))
ROWS, SHOTS = 128, 1024
SUB = 32
HALF = 8 * SUB
WIDE = 2 * ROWS
PEAK = 512.0
TINY = 1e-34
N_SEMS = 142
EV, ET = 126, 134


def kernel(x_ref, o_ref, cols, rows, w, acc0, acc1, enc_out, enc_in, top_out, top_in, ssem, rsem, lsem, ready, mine):
    zlo = lax.axis_index("shot")
    x = lax.axis_index("rr")
    rc = lax.axis_index("rc")
    y = rc // 4
    zhi = (rc // 2) % 2
    c = rc % 2

    def dev(x, y, zhi, zlo, c):
        return {"shot": zlo, "rr": x, "rc": y * 4 + zhi * 2 + c}

    q_odd = zlo + 1 - 2 * (zlo % 2)
    q_two = (zlo + 2) % 4
    q_three = 3 - zlo
    xs = {0: x, 1: (x + 1) % 4, -1: (x + 3) % 4, 2: (x + 2) % 4}
    ys = {0: y, 1: (y + 1) % 4, -1: (y + 3) % 4, 2: (y + 2) % 4}
    xdev = {s: dev(xs[s], y, zhi, zlo, c) for s in (1, -1)}
    ydev = {s: dev(x, ys[s], zhi, zlo, c) for s in (1, -1)}
    shot_pair = dev(x, y, zhi, q_two, c)
    other_half = dev(x, y, 1 - zhi, q_two, c)
    sum_pair = dev(x, y, zhi, q_odd, c)
    sibling = dev(x, y, zhi, zlo, 1 - c)
    near = [xdev[1], xdev[-1], ydev[1], ydev[-1], shot_pair, sum_pair, sibling]

    barrier = pltpu.get_barrier_semaphore()
    for p in near:
        pl.semaphore_signal(barrier, inc=1, device_id=p, device_id_type=MESH)

    @pl.when(zhi == 0)
    def _():
        pl.semaphore_signal(barrier, inc=1, device_id=other_half, device_id_type=MESH)

    pl.semaphore_wait(barrier, len(near) + zhi)

    @pl.when(zhi == 1)
    def _():
        pl.semaphore_signal(ready, inc=1, device_id=other_half, device_id_type=MESH)

    msgs = {}

    def plan(key, src, dst, to):
        i = len(msgs)
        msgs[key] = pltpu.make_async_remote_copy(
            src_ref=src, dst_ref=dst, send_sem=ssem.at[i], recv_sem=rsem.at[i], device_id=to, device_id_type=MESH
        )

    def go(*keys):
        for key in keys:
            msgs[key].start()

    def got(*keys):
        for key in keys:
            msgs[key].wait_recv()

    def part(q):
        return pl.ds(pl.multiple_of(q * SUB, SUB), SUB)

    def strip(zown, yy):
        half = zhi if zown else 1 - zhi
        return half * 8 + ys[yy] * 2 + c

    row_part = (q_odd, zlo)
    there_part = (q_three, q_two)
    order = (q_three, q_odd, q_two, zlo)
    sent_as = (q_odd, q_three, zlo, q_two)
    here = strip(True, 0)

    for i in range(4):
        for p in (0, 1):
            there = cols.at[x, 1, p, part(sent_as[i])]
            plan(("l2", i, p), x_ref.at[p, part(sent_as[i])], there, shot_pair)
    for q in (0, 1):
        for p in (0, 1):
            plan(("zo", q, p), x_ref.at[p, part(there_part[q])], rows.at[q, 1, p, here], other_half)
            plan(("zr", q, p), cols.at[x, 1, p, part(there_part[q])], rows.at[q, 0, p, here], other_half)
    for s in (1, -1):
        handed = 0 if s == 1 else 1
        for p in (0, 1):
            plan(("xd", 0, s, p), x_ref.at[p], cols.at[x, 0, p], xdev[s])
        spot = cols.at[xs[-s], 0, handed]
        plan(("xf", 0, s, 0), spot, spot, xdev[s])
        for i in range(4):
            spot = cols.at[x, 1, :, part(order[i])]
            plan(("xd", 1, s, i), spot, spot, xdev[s])
            spot = cols.at[xs[-s], 1, handed, part(order[i])]
            plan(("xf", 1, s, i), spot, spot, xdev[s])

    def source(zown, g, q, p):
        if not zown:
            return rows.at[q, g, p, strip(zown, 0)]
        return x_ref.at[p, part(row_part[q])] if g == 0 else cols.at[x, 1, p, part(row_part[q])]

    for zown in (True, False):
        for g in (0, 1):
            for q in (0, 1):
                for s in (1, -1):
                    for p in (0, 1):
                        spot = rows.at[q, g, p, strip(zown, 0)]
                        plan(("yd", zown, g, q, s, p), source(zown, g, q, p), spot, ydev[s])
                    p = 0 if s == 1 else 1
                    spot = rows.at[q, g, p, strip(zown, -s)]
                    plan(("yf", zown, g, q, s), spot, spot, ydev[s])
                    spot = rows.at[q, g, p, strip(zown, 2)]
                    plan(("cc", zown, g, q, 2, p), spot, spot, sibling)
                plan(("cc", zown, g, q, 0), source(zown, g, q, slice(None)), rows.at[q, g, :, strip(zown, 0)], sibling)
                for yy in (1, -1):
                    spot = rows.at[q, g, :, strip(zown, yy)]
                    plan(("cc", zown, g, q, yy), spot, spot, sibling)

    own = {
        (g, q): pltpu.make_async_copy(
            x_ref.at[:, part(row_part[q])] if g == 0 else cols.at[x, 1, :, part(row_part[q])],
            rows.at[q, g, :, here],
            lsem.at[g * 2 + q],
        )
        for g in (0, 1)
        for q in (0, 1)
    }

    def y_send(zown, g, q, p):
        go(("yd", zown, g, q, 1, p), ("yd", zown, g, q, -1, p))
        if p == 1:
            go(("cc", zown, g, q, 0))

    def y_forward(zown, g, q):
        for s in (1, -1):
            got(("yd", zown, g, q, s, 0 if s == 1 else 1))
            go(("yf", zown, g, q, s))
        for s in (1, -1):
            got(("yd", zown, g, q, s, 1 if s == 1 else 0))
            go(("cc", zown, g, q, -s))

    def y_last(zown, g, q):
        for s in (1, -1):
            got(("yf", zown, g, q, s))
            go(("cc", zown, g, q, 2, 0 if s == 1 else 1))

    def x_send(i):
        go(("xd", 1, 1, i), ("xd", 1, -1, i))

    def x_forward(i):
        for s in (1, -1):
            got(("xd", 1, s, i))
            go(("xf", 1, s, i))

    def build(d, g, real, imag):
        w[d, g, 0, 0:ROWS] = real
        w[d, g, 0, ROWS:] = -imag
        w[d, g, 1, 0:ROWS] = imag
        w[d, g, 1, ROWS:] = real

    def build_from(d, g, xi):
        build(d, g, cols[xi, g, 0], cols[xi, g, 1])

    def take_sibling(zown, q):
        for g in (0, 1):
            got(*(("cc", zown, g, q, yy) for yy in (0, 1, -1)))
            got(("cc", zown, g, q, 2, 0), ("cc", zown, g, q, 2, 1))

    go(*(("l2", i, p) for i in (0, 1) for p in (0, 1)))

    @pl.when(zhi == 1)
    def _():
        go(("zo", 0, 0), ("zo", 0, 1))

    for p in (0, 1):
        y_send(True, 0, 0, p)
    go(("xd", 0, 1, 0), ("xd", 0, -1, 1), ("xd", 0, 1, 1), ("xd", 0, -1, 0))

    @pl.when(c == 0)
    def _():
        go(*(("l2", i, p) for i in (2, 3) for p in (0, 1)))

    for p in (0, 1):
        y_send(True, 0, 1, p)
    mine_copy = pltpu.make_async_copy(x_ref, mine, lsem.at[4])
    mine_copy.start()
    own[0, 0].start()
    own[0, 1].start()
    mine_copy.wait()
    build(0, 0, mine[0], mine[1])

    y_forward(True, 0, 0)

    @pl.when(c == 1)
    def _():
        go(*(("l2", i, p) for i in (2, 3) for p in (0, 1)))


    @pl.when(zhi == 0)
    def _():
        pl.semaphore_wait(ready, 1)
        go(("zo", 0, 0), ("zo", 0, 1))

    for p in (0, 1):
        got(("zo", 0, p))
        y_send(False, 1, 0, p)
    for p in (0, 1):
        got(("l2", 0, p))
        go(("zr", 0, p))
    go(("zo", 1, 0), ("zo", 1, 1))
    x_send(0)
    y_forward(False, 1, 0)
    y_last(True, 0, 0)
    got(("xd", 0, 1, 0), ("xd", 0, -1, 1))
    go(("xf", 0, 1, 0), ("xf", 0, -1, 0))
    for p in (0, 1):
        got(("l2", 1, p))
        y_send(True, 1, 0, p)
    own[1, 0].start()
    x_send(1)
    for p in (0, 1):
        got(("zr", 0, p))
        y_send(False, 0, 0, p)
    y_last(False, 1, 0)
    y_forward(True, 1, 0)
    got(("xd", 0, 1, 1), ("xd", 0, -1, 0))
    build_from(1, 0, xs[1])
    y_forward(False, 0, 0)
    for p in (0, 1):
        got(("l2", 2, p))
        go(("zr", 1, p))
    x_send(2)
    y_last(True, 1, 0)
    y_forward(True, 0, 1)
    for p in (0, 1):
        got(("zo", 1, p))
        y_send(False, 1, 1, p)
    x_forward(0)
    x_forward(1)
    build_from(2, 0, xs[-1])
    for p in (0, 1):
        got(("l2", 3, p))
        y_send(True, 1, 1, p)
    own[1, 1].start()
    x_send(3)
    build_from(0, 1, x)
    own[0, 0].wait()
    own[1, 0].wait()
    take_sibling(True, 0)

    def before_1():
        y_last(False, 0, 0)
        y_last(True, 0, 1)
        for p in (0, 1):
            got(("zr", 1, p))
            y_send(False, 0, 1, p)
        take_sibling(False, 0)
        y_forward(False, 1, 1)

    def before_2():
        y_forward(True, 1, 1)
        x_forward(2)
        x_forward(3)
        build_from(1, 1, xs[1])

    def before_3():
        y_forward(False, 0, 1)

    def before_4():
        build_from(2, 1, xs[-1])

    def before_5():
        y_last(False, 1, 1)

    def before_6():
        for s in (1, -1):
            got(("xf", 0, s, 0))
            for i in range(4):
                got(("xf", 1, s, i))
        build_from(3, 0, xs[2])
        build_from(3, 1, xs[2])

    def product(left, d):
        total = None
        for g in (0, 1):
            for p in (0, 1):
                term = lax.dot_general(left(g, p), w[d, g, p], NT, preferred_element_type=jnp.float32)
                total = term if total is None else total + term
        return total

    def sums(i):
        copies = []
        for a, b, first in ((enc_out, enc_in, EV), (top_out, top_in, ET)):
            copies.append(
                pltpu.make_async_remote_copy(
                    src_ref=a.at[i],
                    dst_ref=b.at[i],
                    send_sem=ssem.at[first + i],
                    recv_sem=rsem.at[first + i],
                    device_id=sum_pair,
                    device_id_type=MESH,
                )
            )
        return copies

    def give(i, _):
        for k, block in ((1, before_1), (2, before_2), (3, before_3), (4, before_4), (5, before_5), (6, before_6)):
            pl.when(i == k)(block)
        d = i // 2
        half = jnp.where(i % 2 == 0, zhi, 1 - zhi)
        at = pl.ds(half * 8, 8)
        acc0[...] = product(lambda g, p: rows[0, g, p, at].reshape(HALF, SHOTS), d)

        def look(r, top):
            return jnp.maximum(top, jnp.abs(acc0[pl.ds(pl.multiple_of(r * 64, 64), 64)]).reshape(8, 8, WIDE).max(axis=0))

        top = lax.fori_loop(0, 4, look, jnp.zeros((8, WIDE), jnp.float32), unroll=True).max(axis=0, keepdims=True)
        top = jnp.maximum(top, TINY)
        top_out[i] = top
        scale = PEAK / top

        def code(r, _):
            at = pl.ds(pl.multiple_of(r * 64, 64), 64)
            t = acc0[at] * scale
            t2 = t * t
            t4 = t2 * t2
            power = t4 * t4 * t4 * t2
            enc_out[i, at] = jnp.where(t < 0, -power, power).astype(jnp.bfloat16)
            return 0

        lax.fori_loop(0, 4, code, 0, unroll=True)
        for copy in sums(i):
            copy.start()
        return 0

    lax.fori_loop(0, 8, give, 0)

    y_last(True, 1, 1)
    y_last(False, 0, 1)
    own[0, 1].wait()
    own[1, 1].wait()
    take_sibling(True, 1)
    take_sibling(False, 1)

    def keep(d, _):
        acc1[d] = product(lambda g, p: rows[1, g, p].reshape(2 * HALF, SHOTS), d)
        return 0

    lax.fori_loop(0, 4, keep, 0)

    for copy in msgs.values():
        copy.wait_send()

    def finish(i, _):
        for copy in sums(i):
            copy.wait_recv()
        d = i // 2
        half = jnp.where(i % 2 == 0, zhi, 1 - zhi)
        xi = (x + d + (d // 2) * (1 - 2 * (d % 2))) % 4
        top = top_in[i] * (1.0 / PEAK)

        def add(r, _):
            u = enc_in[i, pl.ds(pl.multiple_of(r * 64, 64), 64)].astype(jnp.float32)
            size = jnp.exp2(jnp.log2(jnp.abs(u)) * (1.0 / 14.0)) * top
            at = pl.ds(pl.multiple_of(half * HALF + r * 64, 64), 64)
            total = acc1[d, at] + jnp.where(u < 0, -size, size)
            for k in (0, 1):
                o_ref[pl.ds(k * 2048 + r * 512 + half * 256 + xi, 64, stride=4), :] = total[:, k * ROWS : (k + 1) * ROWS]
            return 0

        lax.fori_loop(0, 4, add, 0, unroll=True)
        return 0

    lax.fori_loop(0, 8, finish, 0)

    def drain(i, _):
        for copy in sums(i):
            copy.wait_send()
        return 0

    lax.fori_loop(0, 8, drain, 0)


def on_device(records):
    flat = pl.pallas_call(
        kernel,
        out_shape=pltpu.VMEM((4096, 128), jnp.float32),
        in_specs=[pl.BlockSpec(memory_space=pltpu.HBM)],
        out_specs=pl.BlockSpec(memory_space=pltpu.VMEM),
        scratch_shapes=[
            pltpu.VMEM((4, 2, 2, ROWS, SHOTS), jnp.bfloat16),
            pltpu.VMEM((2, 2, 2, 16, SUB, SHOTS), jnp.bfloat16),
            pltpu.VMEM((4, 2, 2, WIDE, SHOTS), jnp.bfloat16),
            pltpu.VMEM((HALF, WIDE), jnp.float32),
            pltpu.VMEM((4, 2 * HALF, WIDE), jnp.float32),
            pltpu.VMEM((8, HALF, WIDE), jnp.bfloat16),
            pltpu.VMEM((8, HALF, WIDE), jnp.bfloat16),
            pltpu.VMEM((8, 1, WIDE), jnp.float32),
            pltpu.VMEM((8, 1, WIDE), jnp.float32),
            pltpu.SemaphoreType.DMA((N_SEMS,)),
            pltpu.SemaphoreType.DMA((N_SEMS,)),
            pltpu.SemaphoreType.DMA((5,)),
            pltpu.SemaphoreType.REGULAR,
            pltpu.VMEM((2, ROWS, SHOTS), jnp.bfloat16),
        ],
        compiler_params=pltpu.CompilerParams(
            collective_id=0, has_side_effects=True, vmem_limit_bytes=60 * 2**20
        ),
        cost_estimate=pl.CostEstimate(flops=8_600_000_000, bytes_accessed=3_000_000, transcendentals=1_000_000),
    )(records)
    return flat.reshape(2, 1, 16, 1, 32, 4, 128)


def solution(mesh):
    return jax.shard_map(
        on_device,
        mesh=mesh,
        in_specs=(P(None, ("rr", "rc"), "shot"),),
        out_specs=P(None, "rr", None, "shot", None, None, "rc"),
        check_vma=False,
    )
```

```python
import jax
import jax.numpy as jnp
from jax import lax
from jax.experimental import pallas as pl
from jax.experimental.pallas import tpu as pltpu
from jax.sharding import PartitionSpec as P

MESH = pl.DeviceIdType.MESH
NT = (((1,), (1,)), ((), ()))
ROWS, SHOTS = 128, 1024
SUB = 32
HALF = 8 * SUB
WIDE = 2 * ROWS
PEAK = 512.0
TINY = 1e-34
N_SEMS = 142
EV, ET = 126, 134


def kernel(x_ref, o_ref, cols, rows, w, acc0, acc1, enc_out, enc_in, top_out, top_in, ssem, rsem, lsem, ready, mine):
    zlo = lax.axis_index("shot")
    x = lax.axis_index("rr")
    rc = lax.axis_index("rc")
    y = rc // 4
    zhi = (rc // 2) % 2
    c = rc % 2

    def dev(x, y, zhi, zlo, c):
        return {"shot": zlo, "rr": x, "rc": y * 4 + zhi * 2 + c}

    q_odd = zlo + 1 - 2 * (zlo % 2)
    q_two = (zlo + 2) % 4
    q_three = 3 - zlo
    xs = {0: x, 1: (x + 1) % 4, -1: (x + 3) % 4, 2: (x + 2) % 4}
    ys = {0: y, 1: (y + 1) % 4, -1: (y + 3) % 4, 2: (y + 2) % 4}
    xdev = {s: dev(xs[s], y, zhi, zlo, c) for s in (1, -1)}
    ydev = {s: dev(x, ys[s], zhi, zlo, c) for s in (1, -1)}
    shot_pair = dev(x, y, zhi, q_two, c)
    other_half = dev(x, y, 1 - zhi, q_two, c)
    sum_pair = dev(x, y, zhi, q_odd, c)
    sibling = dev(x, y, zhi, zlo, 1 - c)
    near = [xdev[1], xdev[-1], ydev[1], ydev[-1], shot_pair, sum_pair, sibling]

    barrier = pltpu.get_barrier_semaphore()
    for p in near:
        pl.semaphore_signal(barrier, inc=1, device_id=p, device_id_type=MESH)

    @pl.when(zhi == 0)
    def _():
        pl.semaphore_signal(barrier, inc=1, device_id=other_half, device_id_type=MESH)

    pl.semaphore_wait(barrier, len(near) + zhi)

    @pl.when(zhi == 1)
    def _():
        pl.semaphore_signal(ready, inc=1, device_id=other_half, device_id_type=MESH)

    msgs = {}

    def plan(key, src, dst, to):
        i = len(msgs)
        msgs[key] = pltpu.make_async_remote_copy(
            src_ref=src, dst_ref=dst, send_sem=ssem.at[i], recv_sem=rsem.at[i], device_id=to, device_id_type=MESH
        )

    def go(*keys):
        for key in keys:
            msgs[key].start()

    def got(*keys):
        for key in keys:
            msgs[key].wait_recv()

    def part(q):
        return pl.ds(pl.multiple_of(q * SUB, SUB), SUB)

    def strip(zown, yy):
        half = zhi if zown else 1 - zhi
        return half * 8 + ys[yy] * 2 + c

    row_part = (q_odd, zlo)
    there_part = (q_three, q_two)
    order = (q_three, q_odd, q_two, zlo)
    sent_as = (q_odd, q_three, zlo, q_two)
    here = strip(True, 0)

    for i in range(4):
        for p in (0, 1):
            there = cols.at[x, 1, p, part(sent_as[i])]
            plan(("l2", i, p), x_ref.at[p, part(sent_as[i])], there, shot_pair)
    for q in (0, 1):
        for p in (0, 1):
            plan(("zo", q, p), x_ref.at[p, part(there_part[q])], rows.at[q, 1, p, here], other_half)
            plan(("zr", q, p), cols.at[x, 1, p, part(there_part[q])], rows.at[q, 0, p, here], other_half)
    for s in (1, -1):
        handed = 0 if s == 1 else 1
        for p in (0, 1):
            plan(("xd", 0, s, p), x_ref.at[p], cols.at[x, 0, p], xdev[s])
        spot = cols.at[xs[-s], 0, handed]
        plan(("xf", 0, s, 0), spot, spot, xdev[s])
        for i in range(4):
            spot = cols.at[x, 1, :, part(order[i])]
            plan(("xd", 1, s, i), spot, spot, xdev[s])
            spot = cols.at[xs[-s], 1, handed, part(order[i])]
            plan(("xf", 1, s, i), spot, spot, xdev[s])

    def source(zown, g, q, p):
        if not zown:
            return rows.at[q, g, p, strip(zown, 0)]
        return x_ref.at[p, part(row_part[q])] if g == 0 else cols.at[x, 1, p, part(row_part[q])]

    for zown in (True, False):
        for g in (0, 1):
            for q in (0, 1):
                for s in (1, -1):
                    for p in (0, 1):
                        spot = rows.at[q, g, p, strip(zown, 0)]
                        plan(("yd", zown, g, q, s, p), source(zown, g, q, p), spot, ydev[s])
                    p = 0 if s == 1 else 1
                    spot = rows.at[q, g, p, strip(zown, -s)]
                    plan(("yf", zown, g, q, s), spot, spot, ydev[s])
                    spot = rows.at[q, g, p, strip(zown, 2)]
                    plan(("cc", zown, g, q, 2, p), spot, spot, sibling)
                plan(("cc", zown, g, q, 0), source(zown, g, q, slice(None)), rows.at[q, g, :, strip(zown, 0)], sibling)
                for yy in (1, -1):
                    spot = rows.at[q, g, :, strip(zown, yy)]
                    plan(("cc", zown, g, q, yy), spot, spot, sibling)

    own = {
        (g, q): pltpu.make_async_copy(
            x_ref.at[:, part(row_part[q])] if g == 0 else cols.at[x, 1, :, part(row_part[q])],
            rows.at[q, g, :, here],
            lsem.at[g * 2 + q],
        )
        for g in (0, 1)
        for q in (0, 1)
    }

    def y_send(zown, g, q, p):
        go(("yd", zown, g, q, 1, p), ("yd", zown, g, q, -1, p))
        if p == 1:
            go(("cc", zown, g, q, 0))

    def y_forward(zown, g, q):
        for s in (1, -1):
            got(("yd", zown, g, q, s, 0 if s == 1 else 1))
            go(("yf", zown, g, q, s))
        for s in (1, -1):
            got(("yd", zown, g, q, s, 1 if s == 1 else 0))
            go(("cc", zown, g, q, -s))

    def y_last(zown, g, q):
        for s in (1, -1):
            got(("yf", zown, g, q, s))
            go(("cc", zown, g, q, 2, 0 if s == 1 else 1))

    def x_send(i):
        go(("xd", 1, 1, i), ("xd", 1, -1, i))

    def x_forward(i):
        for s in (1, -1):
            got(("xd", 1, s, i))
            go(("xf", 1, s, i))

    def build(d, g, real, imag):
        w[d, g, 0, 0:ROWS] = real
        w[d, g, 0, ROWS:] = -imag
        w[d, g, 1, 0:ROWS] = imag
        w[d, g, 1, ROWS:] = real

    def build_from(d, g, xi):
        build(d, g, cols[xi, g, 0], cols[xi, g, 1])

    def take_sibling(zown, q):
        for g in (0, 1):
            got(*(("cc", zown, g, q, yy) for yy in (0, 1, -1)))
            got(("cc", zown, g, q, 2, 0), ("cc", zown, g, q, 2, 1))

    go(*(("l2", i, p) for i in (0, 1) for p in (0, 1)))

    @pl.when(zhi == 1)
    def _():
        go(("zo", 0, 0), ("zo", 0, 1))

    for p in (0, 1):
        y_send(True, 0, 0, p)
    go(("xd", 0, 1, 0), ("xd", 0, -1, 1), ("xd", 0, 1, 1), ("xd", 0, -1, 0))

    @pl.when(c == 0)
    def _():
        go(*(("l2", i, p) for i in (2, 3) for p in (0, 1)))

    for p in (0, 1):
        y_send(True, 0, 1, p)
    mine_copy = pltpu.make_async_copy(x_ref, mine, lsem.at[4])
    mine_copy.start()
    own[0, 0].start()
    own[0, 1].start()
    mine_copy.wait()
    build(0, 0, mine[0], mine[1])

    y_forward(True, 0, 0)

    @pl.when(c == 1)
    def _():
        go(*(("l2", i, p) for i in (2, 3) for p in (0, 1)))


    @pl.when(zhi == 0)
    def _():
        pl.semaphore_wait(ready, 1)
        go(("zo", 0, 0), ("zo", 0, 1))

    for p in (0, 1):
        got(("zo", 0, p))
        y_send(False, 1, 0, p)
    for p in (0, 1):
        got(("l2", 0, p))
        go(("zr", 0, p))
    go(("zo", 1, 0), ("zo", 1, 1))
    x_send(0)
    y_forward(False, 1, 0)
    y_last(True, 0, 0)
    y_forward(True, 0, 1)
    got(("xd", 0, 1, 0), ("xd", 0, -1, 1))
    go(("xf", 0, 1, 0), ("xf", 0, -1, 0))
    for p in (0, 1):
        got(("l2", 1, p))
        y_send(True, 1, 0, p)
    own[1, 0].start()
    x_send(1)
    for p in (0, 1):
        got(("zr", 0, p))
        y_send(False, 0, 0, p)
    y_last(False, 1, 0)
    y_forward(True, 1, 0)
    got(("xd", 0, 1, 1), ("xd", 0, -1, 0))
    build_from(1, 0, xs[1])
    y_forward(False, 0, 0)
    for p in (0, 1):
        got(("l2", 2, p))
        go(("zr", 1, p))
    x_send(2)
    y_last(True, 1, 0)
    for p in (0, 1):
        got(("zo", 1, p))
        y_send(False, 1, 1, p)
    x_forward(0)
    x_forward(1)
    build_from(2, 0, xs[-1])
    for p in (0, 1):
        got(("l2", 3, p))
        y_send(True, 1, 1, p)
    own[1, 1].start()
    x_send(3)
    build_from(0, 1, x)
    own[0, 0].wait()
    own[1, 0].wait()
    take_sibling(True, 0)

    def before_1():
        y_last(False, 0, 0)
        y_last(True, 0, 1)
        for p in (0, 1):
            got(("zr", 1, p))
            y_send(False, 0, 1, p)
        take_sibling(False, 0)
        y_forward(False, 1, 1)

    def before_2():
        y_forward(True, 1, 1)
        x_forward(2)
        x_forward(3)
        build_from(1, 1, xs[1])

    def before_3():
        y_forward(False, 0, 1)

    def before_4():
        build_from(2, 1, xs[-1])

    def before_5():
        y_last(False, 1, 1)

    def before_6():
        for s in (1, -1):
            got(("xf", 0, s, 0))
            for i in range(4):
                got(("xf", 1, s, i))
        build_from(3, 0, xs[2])
        build_from(3, 1, xs[2])

    def product(left, d):
        total = None
        for g in (0, 1):
            for p in (0, 1):
                term = lax.dot_general(left(g, p), w[d, g, p], NT, preferred_element_type=jnp.float32)
                total = term if total is None else total + term
        return total

    def sums(i):
        copies = []
        for a, b, first in ((enc_out, enc_in, EV), (top_out, top_in, ET)):
            copies.append(
                pltpu.make_async_remote_copy(
                    src_ref=a.at[i],
                    dst_ref=b.at[i],
                    send_sem=ssem.at[first + i],
                    recv_sem=rsem.at[first + i],
                    device_id=sum_pair,
                    device_id_type=MESH,
                )
            )
        return copies

    def give(i, _):
        for k, block in ((1, before_1), (2, before_2), (3, before_3), (4, before_4), (5, before_5), (6, before_6)):
            pl.when(i == k)(block)
        d = i // 2
        half = jnp.where(i % 2 == 0, zhi, 1 - zhi)
        at = pl.ds(half * 8, 8)
        acc0[...] = product(lambda g, p: rows[0, g, p, at].reshape(HALF, SHOTS), d)

        def look(r, top):
            return jnp.maximum(top, jnp.abs(acc0[pl.ds(pl.multiple_of(r * 64, 64), 64)]).reshape(8, 8, WIDE).max(axis=0))

        top = lax.fori_loop(0, 4, look, jnp.zeros((8, WIDE), jnp.float32), unroll=True).max(axis=0, keepdims=True)
        top = jnp.maximum(top, TINY)
        top_out[i] = top
        scale = PEAK / top

        def code(r, _):
            at = pl.ds(pl.multiple_of(r * 64, 64), 64)
            t = acc0[at] * scale
            t2 = t * t
            t4 = t2 * t2
            power = t4 * t4 * t4 * t2
            enc_out[i, at] = jnp.where(t < 0, -power, power).astype(jnp.bfloat16)
            return 0

        lax.fori_loop(0, 4, code, 0, unroll=True)
        for copy in sums(i):
            copy.start()
        return 0

    lax.fori_loop(0, 8, give, 0)

    y_last(True, 1, 1)
    y_last(False, 0, 1)
    own[0, 1].wait()
    own[1, 1].wait()
    take_sibling(True, 1)
    take_sibling(False, 1)

    def keep(d, _):
        acc1[d] = product(lambda g, p: rows[1, g, p].reshape(2 * HALF, SHOTS), d)
        return 0

    lax.fori_loop(0, 4, keep, 0)

    for copy in msgs.values():
        copy.wait_send()

    def finish(i, _):
        for copy in sums(i):
            copy.wait_recv()
        d = i // 2
        half = jnp.where(i % 2 == 0, zhi, 1 - zhi)
        xi = (x + d + (d // 2) * (1 - 2 * (d % 2))) % 4
        top = top_in[i] * (1.0 / PEAK)

        def add(r, _):
            u = enc_in[i, pl.ds(pl.multiple_of(r * 64, 64), 64)].astype(jnp.float32)
            size = jnp.exp2(jnp.log2(jnp.abs(u)) * (1.0 / 14.0)) * top
            at = pl.ds(pl.multiple_of(half * HALF + r * 64, 64), 64)
            total = acc1[d, at] + jnp.where(u < 0, -size, size)
            for k in (0, 1):
                o_ref[pl.ds(k * 2048 + r * 512 + half * 256 + xi, 64, stride=4), :] = total[:, k * ROWS : (k + 1) * ROWS]
            return 0

        lax.fori_loop(0, 4, add, 0, unroll=True)
        return 0

    lax.fori_loop(0, 8, finish, 0)

    def drain(i, _):
        for copy in sums(i):
            copy.wait_send()
        return 0

    lax.fori_loop(0, 8, drain, 0)


def on_device(records):
    flat = pl.pallas_call(
        kernel,
        out_shape=pltpu.VMEM((4096, 128), jnp.float32),
        in_specs=[pl.BlockSpec(memory_space=pltpu.HBM)],
        out_specs=pl.BlockSpec(memory_space=pltpu.VMEM),
        scratch_shapes=[
            pltpu.VMEM((4, 2, 2, ROWS, SHOTS), jnp.bfloat16),
            pltpu.VMEM((2, 2, 2, 16, SUB, SHOTS), jnp.bfloat16),
            pltpu.VMEM((4, 2, 2, WIDE, SHOTS), jnp.bfloat16),
            pltpu.VMEM((HALF, WIDE), jnp.float32),
            pltpu.VMEM((4, 2 * HALF, WIDE), jnp.float32),
            pltpu.VMEM((8, HALF, WIDE), jnp.bfloat16),
            pltpu.VMEM((8, HALF, WIDE), jnp.bfloat16),
            pltpu.VMEM((8, 1, WIDE), jnp.float32),
            pltpu.VMEM((8, 1, WIDE), jnp.float32),
            pltpu.SemaphoreType.DMA((N_SEMS,)),
            pltpu.SemaphoreType.DMA((N_SEMS,)),
            pltpu.SemaphoreType.DMA((5,)),
            pltpu.SemaphoreType.REGULAR,
            pltpu.VMEM((2, ROWS, SHOTS), jnp.bfloat16),
        ],
        compiler_params=pltpu.CompilerParams(
            collective_id=0, has_side_effects=True, vmem_limit_bytes=60 * 2**20
        ),
        cost_estimate=pl.CostEstimate(flops=8_600_000_000, bytes_accessed=3_000_000, transcendentals=1_000_000),
    )(records)
    return flat.reshape(2, 1, 16, 1, 32, 4, 128)


def solution(mesh):
    return jax.shard_map(
        on_device,
        mesh=mesh,
        in_specs=(P(None, ("rr", "rc"), "shot"),),
        out_specs=P(None, "rr", None, "shot", None, None, "rc"),
        check_vma=False,
    )
```
